256 devices in a mesh: member: 16 (over x, y), band: 16 (over z, core).
Axes of the slice: x: 4, y: 4, z: 8, core: 2. Of those that a mesh axis runs over, the one named last changes fastest.
Arguments:
- perturb: bfloat16 [80, 2, 16, 131072], P('member', None, None, 'band'), may hold values from -15 to 15
- control: float32 [2, 16, 131072], P(None, None, 'band'), may hold values from -6 to 6
- static_cov: float32 [2, 16, 16], replicated, may hold values from -1.5 to 1.5
- loc_table: bfloat16 [16, 256, 256], replicated, may hold values from -0.109375 to 0.109375
- pair_offset: int32 [512, 12], P('band'), may hold values from -6 to 6, as said below
- pair_table: int32 [512, 12], P('band'), may hold values from 0 to 15
- pair_count: int32 [512], P('band'), may hold values from 1 to 12, as said below
Outputs:
- increment: float32 [2, 16, 131072], P(None, 'member', 'band')
The draws below stay inside these ranges and needn't reach their ends.
Inputs may be any that keep to these rules, and one draw needn't show every extreme that they name: `pair_offset`: the offsets of one block are distinct. `pair_count`: counting blocks in aligned runs of 32, the first 6 and the last 6 blocks of every run have all 12 slots live; so do all blocks of some runs, the first run among them.
All inputs are finite; a program needn't handle non-finite values.
Results may differ from the reference program's by a relative error of at most 0.0022.
Values may be sent and summed in bfloat16 or wider, within the bound.
No kernel may reach another device: no remote copies, remote signals or barrier semaphores. Data moves between devices by JAX's collectives and lax.ppermute only.
A program may use at most 128 MiB of HBM per device.

```python
import jax
import jax.numpy as jnp
from jax import lax

K = 80
F = 2
LEV = 16
COLS = 256
BLK_DEV = 32
HB = 6
PMAX = 12
NTAB = 16
NB = 512
NCOL = 131072


def draw_pair_offset(key, part):
    key = jax.random.fold_in(key, 11)
    width = 2 * HB + 1
    scores = jax.random.randint(key, (NB, width), 0, 1 << 20) * width + jnp.arange(width, dtype=jnp.int32)[None, :]
    order = jnp.argsort(scores, axis=1, stable=True)
    return (order[:, :PMAX] - HB).astype(jnp.int32)


def draw_pair_count(key, part):
    key = jax.random.fold_in(key, 23)
    first, second = jax.random.split(key)
    base = jax.random.randint(first, (NB,), 1, PMAX + 1)
    busy = jax.random.randint(second, (NB // BLK_DEV,), 0, 4) == 0
    busy = busy.at[0].set(True)
    busy = jnp.repeat(busy, BLK_DEV)
    inner = jnp.arange(NB, dtype=jnp.int32) % BLK_DEV
    edge = (inner < HB) | (inner >= BLK_DEV - HB)
    return jnp.where(busy | edge, PMAX, base).astype(jnp.int32)


def with_ends(entries, own_key, low, largest):
    index_at = [jax.random.randint(jax.random.fold_in(own_key, axis), (), 0, length) for axis, length in enumerate(entries.shape)]
    longest = entries.shape.index(max(entries.shape))
    beside = index_at[:longest] + [(index_at[longest] + 1) % entries.shape[longest]] + index_at[longest + 1:]
    return entries.at[tuple(index_at)].set(low).at[tuple(beside)].set(largest)


def steps_of(key, extent, cuts, low, high):
    def one(dim, blocks):
        steps = jax.random.uniform(jax.random.fold_in(jax.random.fold_in(key, 6), dim), (blocks,), jnp.float32, low / len(cuts), high / len(cuts))
        return jnp.repeat(jnp.exp(steps), extent[dim] // blocks).reshape((-1,) + (1,) * (len(extent) - dim - 1))

    factor_of = one(*cuts[0])
    for cut in cuts[1:]:
        factor_of = factor_of * one(*cut)
    return factor_of


def scatter_about(stream_key, shape, scale, bound, pieces=(), kind=jnp.bfloat16):
    entries = jax.random.normal(stream_key, shape, jnp.float32) * scale
    if len(pieces) > 0:
        entries = steps_of(stream_key, shape, pieces, -0.22, 0.18) * entries
    return jnp.clip(entries, min=-bound, max=bound).astype(kind)


def setup_inputs(seed: int = 0) -> dict:
    arg_keys = jax.random.split(jax.random.key(seed), 8)
    return {
        "perturb": scatter_about(arg_keys[0], (K, F, LEV, NCOL), 3.0, 15.0, ((0, 16), (3, 16))),
        "control": scatter_about(arg_keys[1], (F, LEV, NCOL), 1.0, 6.0, ((2, 16),), jnp.float32),
        "static_cov": scatter_about(arg_keys[2], (F, LEV, LEV), LEV ** -0.5, 1.5, (), jnp.float32),
        "loc_table": scatter_about(arg_keys[3], (NTAB, COLS, COLS), (COLS * PMAX) ** -0.5, 0.109375),
        "pair_offset": draw_pair_offset(jax.random.fold_in(arg_keys[7], 71), 0),
        "pair_table": with_ends(jax.random.randint(arg_keys[5], (NB, PMAX), 0, NTAB), jax.random.fold_in(arg_keys[5], 1), 0, NTAB - 1).astype(jnp.int32),
        "pair_count": draw_pair_count(jax.random.fold_in(arg_keys[7], 71), 0),
    }


def reference(perturb, control, static_cov, loc_table, pair_offset, pair_table, pair_count):
    nblk = NCOL // COLS
    rows = K * F * LEV
    words = (perturb.astype(jnp.float32) * control[None]).astype(jnp.bfloat16)
    blocks = words.reshape(rows, nblk, COLS)
    slots = jnp.arange(PMAX).astype(jnp.int32)

    def one_block(index):
        partner = ((index + pair_offset[index]) % nblk).astype(jnp.int32)
        picked = blocks[:, partner, :].astype(jnp.float32)
        tables = loc_table[pair_table[index]].astype(jnp.float32)
        prod = jnp.einsum("rpi,pij->rpj", picked, tables)
        live = (slots < pair_count[index]).astype(jnp.float32)
        return jnp.einsum("rpj,p->rj", prod, live)

    spread = lax.map(one_block, jnp.arange(nblk).astype(jnp.int32))
    spread = jnp.transpose(spread, (1, 0, 2)).reshape(K, F, LEV, NCOL)
    ensemble = jnp.sum(perturb.astype(jnp.float32) * spread, axis=0) / (K - 1)
    static = jnp.einsum("fml,flc->fmc", static_cov, control, precision=lax.Precision.HIGHEST)
    return 0.5 * static + 0.5 * ensemble
```

```python
import functools

import jax
import jax.numpy as jnp
from jax import lax
from jax.experimental import pallas as pl
from jax.experimental.pallas import tpu as pltpu
from jax.sharding import PartitionSpec as P

HB = 6
COLS = 256
LANES = 128


def fetch(copies):
    for copy in copies:
        copy.start()
    for copy in copies:
        copy.wait()


def block_term(b, nslots, zero_block, offs, tabs, cnts, words, tables, perturb, part, scale):
    count = cnts[b]
    acc = None
    for s in range(nslots):
        c = jnp.where(s < count, HB + b + offs[b, s], zero_block)
        lhs = words[:, pl.ds(pl.multiple_of(c * COLS, COLS), COLS)]
        prod = jnp.dot(lhs, tables[tabs[b, s]], preferred_element_type=jnp.float32)
        acc = prod if acc is None else acc + prod
    cols = pl.ds(pl.multiple_of(b * COLS, COLS), COLS)
    members = perturb.shape[0]
    fl = perturb.shape[1]
    total = None
    for k in range(members):
        term = perturb[k, :, cols].astype(jnp.float32) * acc[k * fl : (k + 1) * fl]
        total = term if total is None else total + term
    total = total * scale
    rows_per_level = part.shape[0] // 16
    per_field = rows_per_level // 2
    for f in range(2):
        for l0 in (0, 8):
            for h in range(COLS // LANES):
                r = f * 16 + l0
                start = l0 * rows_per_level + f * per_field + (COLS // LANES) * b + h
                part[pl.ds(start, 8, stride=rows_per_level), :] = total[
                    r : r + 8, h * LANES : (h + 1) * LANES
                ]


def inner_kernel(
    scale, member, cov, offs_in, tabs_in, cnts_in, perturb, control, tables,
    words, part, static, offs, tabs, cnts, sems,
):
    fetch([
        pltpu.make_async_copy(offs_in, offs, sems.at[0]),
        pltpu.make_async_copy(tabs_in, tabs, sems.at[1]),
        pltpu.make_async_copy(cnts_in, cnts, sems.at[2]),
    ])
    members, fl, width = perturb.shape
    nblk = width // COLS
    zero_block = nblk + 2 * HB
    words[:, zero_block * COLS : (zero_block + 1) * COLS] = jnp.zeros(
        (words.shape[0], COLS), words.dtype
    )
    row = lax.broadcasted_iota(jnp.int32, (fl, LANES), 0)
    me = member[0]
    weights = jnp.zeros((fl, LANES), jnp.float32)
    for f in range(2):
        for l in range(16):
            weights = jnp.where(row == f * 16 + l, 0.5 * cov[f, me * 16 + l], weights)
    per_field = static.shape[0] // 2

    def form(b, carry):
        for h in range(COLS // LANES):
            cols = pl.ds(pl.multiple_of(b * COLS + h * LANES, LANES), LANES)
            dst = pl.ds(pl.multiple_of((HB + b) * COLS + h * LANES, LANES), LANES)
            ctl = control[:, cols]
            for k in range(members):
                words[k * fl : (k + 1) * fl, dst] = (
                    perturb[k, :, cols].astype(jnp.float32) * ctl
                ).astype(jnp.bfloat16)
            own = weights * ctl
            for f in range(2):
                line = jnp.sum(own[f * 16 : (f + 1) * 16], axis=0, keepdims=True)
                static[pl.ds(f * per_field + (COLS // LANES) * b + h, 1), :] = line
        return carry

    lax.fori_loop(0, nblk, form, 0)

    def step(i, carry):
        for u in range(4):
            block_term(
                HB + i * 4 + u, offs.shape[1], zero_block, offs, tabs, cnts,
                words, tables, perturb, part, scale,
            )
        return carry

    lax.fori_loop(0, (nblk - 2 * HB) // 4, step, 0)


def edge_kernel(
    scale, offs_in, tabs_in, cnts_in, left, right, perturb, tables, words_in, part_in,
    out, words, part, offs, tabs, cnts, sems,
):
    del words_in, part_in
    members, fl, width = perturb.shape
    nblk = width // COLS
    zero_block = nblk + 2 * HB
    fetch([
        pltpu.make_async_copy(offs_in, offs, sems.at[0]),
        pltpu.make_async_copy(tabs_in, tabs, sems.at[1]),
        pltpu.make_async_copy(cnts_in, cnts, sems.at[2]),
        pltpu.make_async_copy(left, words.at[:, pl.ds(0, HB * COLS)], sems.at[3]),
        pltpu.make_async_copy(
            right, words.at[:, pl.ds((HB + nblk) * COLS, HB * COLS)], sems.at[4]
        ),
    ])

    def step(i, carry):
        for u in range(HB):
            block_term(
                i * (nblk - HB) + u, offs.shape[1], zero_block, offs, tabs, cnts,
                words, tables, perturb, part, scale,
            )
        return carry

    lax.fori_loop(0, 2, step, 0)
    rows = out.shape[1]

    def pack(m, carry):
        out[m] = part[pl.ds(pl.multiple_of(m * rows, rows), rows), :].astype(out.dtype)
        return carry

    lax.fori_loop(0, out.shape[0], pack, 0)


def per_device(perturb, control, static_cov, loc_table, pair_offset, pair_table, pair_count):
    groups = lax.axis_size("member")
    bands = lax.axis_size("band")
    members, fields, levels, width = perturb.shape
    fl = fields * levels
    nblk = width // COLS
    slots = pair_offset.shape[1]
    lines = fields * width // LANES
    scale = 0.5 / (members * groups - 1)
    perturb = perturb.reshape(members, fl, width)
    control = control.reshape(fl, width)
    edge = HB * COLS

    def form(lo):
        p = lax.slice_in_dim(perturb, lo, lo + edge, axis=2).astype(jnp.float32)
        c = lax.slice_in_dim(control, lo, lo + edge, axis=1)
        return (p * c[None]).astype(jnp.bfloat16).reshape(members * fl, edge)

    up = [(i, (i + 1) % bands) for i in range(bands)]
    down = [((i + 1) % bands, i) for i in range(bands)]
    left = lax.ppermute(form(width - edge), "band", up)
    right = lax.ppermute(form(0), "band", down)

    me = lax.axis_index("member").astype(jnp.int32).reshape(1)
    vmem = pl.BlockSpec(memory_space=pltpu.VMEM)
    smem = pl.BlockSpec(memory_space=pltpu.SMEM)
    anym = pl.BlockSpec(memory_space=pl.ANY)
    tables_scratch = [
        pltpu.SMEM((nblk, slots), jnp.int32),
        pltpu.SMEM((nblk, slots), jnp.int32),
        pltpu.SMEM((nblk,), jnp.int32),
    ]
    words_shape = jax.ShapeDtypeStruct((members * fl, (nblk + 2 * HB + 1) * COLS), jnp.bfloat16)
    part_shape = jax.ShapeDtypeStruct((levels * lines, LANES), jnp.float32)
    words, part, static = pl.pallas_call(
        functools.partial(inner_kernel, scale),
        out_shape=(words_shape, part_shape, jax.ShapeDtypeStruct((lines, LANES), jnp.float32)),
        in_specs=[smem, smem, anym, anym, anym, vmem, vmem, vmem],
        out_specs=(vmem, vmem, vmem),
        scratch_shapes=tables_scratch + [pltpu.SemaphoreType.DMA((3,))],
        compiler_params=pltpu.CompilerParams(vmem_limit_bytes=32 * 2**20),
        cost_estimate=pl.CostEstimate(
            flops=2 * members * fl * COLS * COLS * slots * (nblk - 2 * HB),
            bytes_accessed=12 * 2**20, transcendentals=0,
        ),
    )(
        me, static_cov.reshape(fields, levels * levels), pair_offset, pair_table, pair_count,
        perturb, control, loc_table,
    )
    partial, _, _ = pl.pallas_call(
        functools.partial(edge_kernel, scale),
        out_shape=(
            jax.ShapeDtypeStruct((levels, lines, LANES), jnp.bfloat16), words_shape, part_shape
        ),
        in_specs=[anym] * 5 + [vmem] * 4,
        out_specs=(vmem, vmem, vmem),
        scratch_shapes=tables_scratch + [pltpu.SemaphoreType.DMA((5,))],
        input_output_aliases={7: 1, 8: 2},
        compiler_params=pltpu.CompilerParams(vmem_limit_bytes=32 * 2**20),
        cost_estimate=pl.CostEstimate(
            flops=2 * members * fl * COLS * COLS * slots * 2 * HB,
            bytes_accessed=8 * 2**20, transcendentals=0,
        ),
    )(pair_offset, pair_table, pair_count, left, right, perturb, loc_table, words, part)
    owned = lax.all_to_all(partial, "member", split_axis=0, concat_axis=0, tiled=True)
    total = jnp.sum(owned.astype(jnp.float32), axis=0) + static
    return total.reshape(fields, 1, width)


def solution(mesh):
    return jax.shard_map(
        per_device,
        mesh=mesh,
        in_specs=(
            P("member", None, None, "band"),
            P(None, None, "band"),
            P(),
            P(),
            P("band", None),
            P("band", None),
            P("band"),
        ),
        out_specs=P(None, "member", "band"),
        check_vma=False,
    )
```

```python
import functools

import jax
import jax.numpy as jnp
from jax import lax
from jax.experimental import pallas as pl
from jax.experimental.pallas import tpu as pltpu
from jax.sharding import PartitionSpec as P

HB = 6
COLS = 256
LANES = 128
HALVES = COLS // LANES
LOAD_MIB = 16


def form_words(perturb, control, cols):
    members, fl = perturb.shape[0], perturb.shape[1]
    ctl = control[:, cols]
    return [
        (slice(k * fl, (k + 1) * fl), (perturb[k, :, cols].astype(jnp.float32) * ctl).astype(jnp.bfloat16))
        for k in range(members)
    ]


def block_term(b, zero_block, offs, tabs, cnts, words, tables, perturb, part, scale):
    count = cnts[b]
    acc = None
    for s in range(offs.shape[0]):
        c = jnp.where(s < count, HB + b + offs[s, b], zero_block)
        lhs = words[:, pl.ds(pl.multiple_of(c * COLS, COLS), COLS)]
        prod = jnp.dot(lhs, tables[tabs[s, b]], preferred_element_type=jnp.float32)
        acc = prod if acc is None else acc + prod
    cols = pl.ds(pl.multiple_of(b * COLS, COLS), COLS)
    members, fl = perturb.shape[0], perturb.shape[1]
    total = None
    for k in range(members):
        term = perturb[k, :, cols].astype(jnp.float32) * acc[k * fl : (k + 1) * fl]
        total = term if total is None else total + term
    total = total * scale
    lines = part.shape[0] // 16
    for f in range(2):
        for l0 in (0, 8):
            for h in range(HALVES):
                r = f * 16 + l0
                start = l0 * lines + f * (lines // 2) + HALVES * b + h
                part[pl.ds(start, 8, stride=lines), :] = total[
                    r : r + 8, h * LANES : (h + 1) * LANES
                ]


def load_kernel(
    perturb_in, control_in, tables_in, head, tail, words, perturb, control, tables, sems
):
    edge = head.shape[1]
    members, fl, width = perturb.shape
    nblk = width // COLS
    chunk = 4 * COLS
    starts = [(0, edge), (width - edge, edge)]
    starts += [(lo, chunk) for lo in range(edge, width - edge, chunk)]
    pieces = []
    for lo, size in starts:
        at = pl.ds(lo, size)
        pieces.append((perturb_in.at[:, :, at], perturb.at[:, :, at]))
        pieces.append((control_in.at[:, at], control.at[:, at]))
    half = tables.shape[0] // 2
    for i in range(2):
        pieces.append((tables_in.at[pl.ds(i * half, half)], tables.at[pl.ds(i * half, half)]))
    copies = [pltpu.make_async_copy(src, dst, sems.at[i]) for i, (src, dst) in enumerate(pieces)]
    for copy in copies:
        copy.start()
    zero = (nblk + 2 * HB) * COLS
    words[:, zero : zero + COLS] = jnp.zeros((words.shape[0], COLS), words.dtype)
    for i, (lo, size) in enumerate(starts):
        copies[2 * i].wait()
        copies[2 * i + 1].wait()

        def form(j, carry, i=i, lo=lo):
            cols = pl.ds(pl.multiple_of(lo + j * LANES, LANES), LANES)
            dst = pl.ds(pl.multiple_of(edge + lo + j * LANES, LANES), LANES)
            for rows, value in form_words(perturb, control, cols):
                words[rows, dst] = value
                if i < 2:
                    send = (head, tail)[i]
                    send[rows, pl.ds(pl.multiple_of(j * LANES, LANES), LANES)] = value
            return carry

        lax.fori_loop(0, size // LANES, form, 0, unroll=2)
    for copy in copies[2 * len(starts) :]:
        copy.wait()


def inner_kernel(
    scale, offs_in, tabs_in, cnts_in, cov_in, words, perturb, control, tables,
    part, static, offs, tabs, cnts, cov, sems,
):
    copies = [
        pltpu.make_async_copy(src, dst, sems.at[i])
        for i, (src, dst) in enumerate(
            ((offs_in, offs), (tabs_in, tabs), (cnts_in, cnts), (cov_in, cov))
        )
    ]
    for copy in copies:
        copy.start()
    _, fl, width = perturb.shape
    nblk = width // COLS
    for copy in copies:
        copy.wait()

    def step(i, carry):
        for u in range(4):
            block_term(
                HB + i * 4 + u, nblk + 2 * HB, offs, tabs, cnts,
                words, tables, perturb, part, scale,
            )
        return carry

    lax.fori_loop(0, (nblk - 2 * HB) // 4, step, 0)

    row = lax.broadcasted_iota(jnp.int32, (fl, LANES), 0)
    me = lax.axis_index("member")
    weights = jnp.zeros((fl, LANES), jnp.float32)
    for f in range(2):
        for l in range(16):
            weights = jnp.where(row == f * 16 + l, 0.5 * cov[f * 16 + me, l], weights)
    lines = static.shape[0]

    def static_line(b, carry):
        for h in range(HALVES):
            own = weights * control[:, pl.ds(pl.multiple_of(b * COLS + h * LANES, LANES), LANES)]
            for f in range(2):
                line = jnp.sum(own[f * 16 : (f + 1) * 16], axis=0, keepdims=True)
                static[pl.ds(f * (lines // 2) + HALVES * b + h, 1), :] = line
        return carry

    lax.fori_loop(0, nblk, static_line, 0, unroll=4)


def edge_kernel(
    scale, offs_in, tabs_in, cnts_in, left, right, perturb, tables, words_in, part_in,
    out, words, part, offs, tabs, cnts, sems,
):
    del words_in, part_in
    copies = [
        pltpu.make_async_copy(src, dst, sems.at[i])
        for i, (src, dst) in enumerate(((offs_in, offs), (tabs_in, tabs), (cnts_in, cnts)))
    ]
    for copy in copies:
        copy.start()
    width = perturb.shape[2]
    nblk = width // COLS
    edge = HB * COLS
    zero_block = nblk + 2 * HB
    words[:, 0:edge] = left[...]
    words[:, width + edge : width + 2 * edge] = right[...]
    for copy in copies:
        copy.wait()

    def step(i, carry):
        for u in range(HB):
            block_term(
                i * (nblk - HB) + u, zero_block, offs, tabs, cnts,
                words, tables, perturb, part, scale,
            )
        return carry

    lax.fori_loop(0, 2, step, 0)
    rows = out.shape[1]

    def pack(m, carry):
        out[m] = part[pl.ds(pl.multiple_of(m * rows, rows), rows), :].astype(out.dtype)
        return carry

    lax.fori_loop(0, out.shape[0], pack, 0, unroll=2)


VMEM = pl.BlockSpec(memory_space=pltpu.VMEM)
ANY = pl.BlockSpec(memory_space=pl.ANY)


def params(mib):
    return pltpu.CompilerParams(vmem_limit_bytes=mib * 2**20)


def cost(flops, nbytes):
    return pl.CostEstimate(flops=flops, bytes_accessed=nbytes, transcendentals=0)


def like(array):
    return pltpu.VMEM(array.shape, array.dtype)


def load(perturb, control, tables):
    members, fl, width = perturb.shape
    edge = HB * COLS
    send = pltpu.VMEM((members * fl, edge), jnp.bfloat16)
    words = pltpu.VMEM((members * fl, width + 2 * edge + COLS), jnp.bfloat16)
    return pl.pallas_call(
        load_kernel,
        out_shape=(send, send, words, like(perturb), like(control), like(tables)),
        in_specs=[ANY] * 3,
        out_specs=(VMEM,) * 6,
        scratch_shapes=[pltpu.SemaphoreType.DMA((2 * (2 + (width - 2 * edge) // (4 * COLS)) + 2,))],
        compiler_params=params(LOAD_MIB),
        cost_estimate=cost(10**6, 12 * 2**20),
    )(*(pltpu.with_memory_space_constraint(x, pltpu.HBM) for x in (perturb, control, tables)))


def index_scratch(offs, cnts):
    return [
        pltpu.SMEM(offs.shape, jnp.int32),
        pltpu.SMEM(offs.shape, jnp.int32),
        pltpu.SMEM(cnts.shape, jnp.int32),
    ]


def inner_blocks(scale, levels, offs, tabs, cnts, cov, words, perturb, control, tables):
    members, fl, width = perturb.shape
    nblk = width // COLS
    lines = fl // levels * width // LANES
    return pl.pallas_call(
        functools.partial(inner_kernel, scale),
        out_shape=(
            pltpu.VMEM((levels * lines, LANES), jnp.float32),
            pltpu.VMEM((lines, LANES), jnp.float32),
        ),
        in_specs=[ANY] * 4 + [VMEM] * 4,
        out_specs=(VMEM, VMEM),
        scratch_shapes=index_scratch(offs, cnts)
        + [pltpu.SMEM(cov.shape, jnp.float32), pltpu.SemaphoreType.DMA((4,))],
        compiler_params=params(16),
        cost_estimate=cost(2 * members * fl * COLS**2 * offs.shape[0] * (nblk - 2 * HB), 12 * 2**20),
    )(offs, tabs, cnts, cov, words, perturb, control, tables)


def edge_blocks(scale, levels, offs, tabs, cnts, left, right, perturb, tables, words, part):
    members, fl, width = perturb.shape
    lines = fl // levels * width // LANES
    return pl.pallas_call(
        functools.partial(edge_kernel, scale),
        out_shape=(
            pltpu.VMEM((levels, lines, LANES), jnp.bfloat16),
            like(words),
            like(part),
        ),
        in_specs=[ANY] * 3 + [VMEM] * 6,
        out_specs=(VMEM, VMEM, VMEM),
        scratch_shapes=index_scratch(offs, cnts) + [pltpu.SemaphoreType.DMA((3,))],
        input_output_aliases={7: 1, 8: 2},
        compiler_params=params(16),
        cost_estimate=cost(2 * members * fl * COLS**2 * offs.shape[0] * 2 * HB, 8 * 2**20),
    )(offs, tabs, cnts, left, right, perturb, tables, words, part)[0]


def per_device(perturb, control, static_cov, loc_table, pair_offset, pair_table, pair_count):
    groups = lax.axis_size("member")
    bands = lax.axis_size("band")
    members, fields, levels, width = perturb.shape
    scale = 0.5 / (members * groups - 1)
    perturb = perturb.reshape(members, fields * levels, width)
    control = control.reshape(fields * levels, width)
    cov = static_cov.reshape(fields * levels, levels)
    offs, tabs = pair_offset.T, pair_table.T

    head, tail, words, perturb, control, tables = load(perturb, control, loc_table)
    up = [(i, (i + 1) % bands) for i in range(bands)]
    down = [((i + 1) % bands, i) for i in range(bands)]
    left = lax.ppermute(tail, "band", up)
    right = lax.ppermute(head, "band", down)
    part, static = inner_blocks(
        scale, levels, offs, tabs, pair_count, cov, words, perturb, control, tables
    )
    partial = edge_blocks(
        scale, levels, offs, tabs, pair_count, left, right, perturb, tables, words, part
    )
    owned = lax.all_to_all(partial, "member", split_axis=0, concat_axis=0, tiled=True)
    total = jnp.sum(owned.astype(jnp.float32), axis=0) + static
    return total.reshape(fields, 1, width)


def solution(mesh):
    return jax.shard_map(
        per_device,
        mesh=mesh,
        in_specs=(
            P("member", None, None, "band"),
            P(None, None, "band"),
            P(),
            P(),
            P("band", None),
            P("band", None),
            P("band"),
        ),
        out_specs=P(None, "member", "band"),
        check_vma=False,
    )
```

```python
import functools

import jax
import jax.numpy as jnp
from jax import lax
from jax.experimental import pallas as pl
from jax.experimental.pallas import tpu as pltpu
from jax.sharding import PartitionSpec as P

HB = 6
COLS = 256
LANES = 128
HALVES = COLS // LANES
INNER_RUN = 10


def form_words(perturb, control, cols):
    members, fl = perturb.shape[0], perturb.shape[1]
    ctl = control[:, cols]
    return [
        (slice(k * fl, (k + 1) * fl), (perturb[k, :, cols].astype(jnp.float32) * ctl).astype(jnp.bfloat16))
        for k in range(members)
    ]


def block_term(b, zero_block, offs, tabs, cnts, words, tables, perturb, part, scale):
    count = cnts[b]
    acc = None
    for s in range(offs.shape[0]):
        c = jnp.where(s < count, HB + b + offs[s, b], zero_block)
        lhs = words[:, pl.ds(pl.multiple_of(c * COLS, COLS), COLS)]
        prod = jnp.dot(lhs, tables[tabs[s, b]], preferred_element_type=jnp.float32)
        acc = prod if acc is None else acc + prod
    cols = pl.ds(pl.multiple_of(b * COLS, COLS), COLS)
    members, fl = perturb.shape[0], perturb.shape[1]
    total = None
    for k in range(members):
        term = perturb[k, :, cols].astype(jnp.float32) * acc[k * fl : (k + 1) * fl]
        total = term if total is None else total + term
    total = total * scale
    for h in range(HALVES):
        part[HALVES * b + h] = total[:, h * LANES : (h + 1) * LANES]


def far_is_left():
    return lax.axis_index("band") % 2 == 0


def start_all(sems, pairs):
    copies = [pltpu.make_async_copy(src, dst, sems.at[i]) for i, (src, dst) in enumerate(pairs)]
    for copy in copies:
        copy.start()
    return copies


def load_kernel(
    perturb_in, control_in, tables_in, offs_in, tabs_in, cnts_in, cov_in,
    far, near, words, perturb, control, tables, offs, tabs, cnts, cov, sems,
):
    edge = HB * COLS
    _, _, width = perturb.shape
    chunk = 4 * COLS
    left = far_is_left()
    far_lo = pl.multiple_of(jnp.where(left, 0, width - edge), LANES)
    near_lo = pl.multiple_of(jnp.where(left, width - edge, 0), LANES)
    starts = [(far_lo, edge), (near_lo, edge)]
    starts += [(lo, chunk) for lo in range(edge, width - edge, chunk)]
    pairs = []
    for lo, size in starts:
        at = pl.ds(lo, size)
        pairs.append((perturb_in.at[:, :, at], perturb.at[:, :, at]))
        pairs.append((control_in.at[:, at], control.at[:, at]))
    half = tables.shape[0] // 2
    for i in range(2):
        pairs.append((tables_in.at[pl.ds(i * half, half)], tables.at[pl.ds(i * half, half)]))
    pairs += [(offs_in, offs), (tabs_in, tabs), (cnts_in, cnts), (cov_in, cov)]
    copies = start_all(sems, pairs)
    zero = width + 2 * edge
    words[:, zero : zero + COLS] = jnp.zeros((words.shape[0], COLS), words.dtype)
    for i, (lo, size) in enumerate(starts):
        copies[2 * i].wait()
        copies[2 * i + 1].wait()

        def form(j, carry, i=i, lo=lo):
            cols = pl.ds(pl.multiple_of(lo + j * LANES, LANES), LANES)
            dst = pl.ds(pl.multiple_of(edge + lo + j * LANES, LANES), LANES)
            for rows, value in form_words(perturb, control, cols):
                words[rows, dst] = value
                if i < 2:
                    send = (far, near)[i]
                    send[rows, pl.ds(pl.multiple_of(j * LANES, LANES), LANES)] = value
            return carry

        lax.fori_loop(0, size // LANES, form, 0, unroll=2)
    for copy in copies[2 * len(starts) :]:
        copy.wait()


def inner_kernel(
    scale, offs, tabs, cnts, cov, words, perturb, control, tables, part, static
):
    _, fl, width = perturb.shape
    nblk = width // COLS
    inner = nblk - 2 * HB
    run = INNER_RUN

    def step(i, carry):
        for u in range(run):
            block_term(
                HB + i * run + u, nblk + 2 * HB, offs, tabs, cnts,
                words, tables, perturb, part, scale,
            )
        return carry

    lax.fori_loop(0, inner // run, step, 0)

    row = lax.broadcasted_iota(jnp.int32, (fl, LANES), 0)
    me = lax.axis_index("member")
    weights = jnp.zeros((fl, LANES), jnp.float32)
    for f in range(2):
        for l in range(16):
            weights = jnp.where(row == f * 16 + l, 0.5 * cov[f * 16 + me, l], weights)
    lines = static.shape[0]

    def static_line(b, carry):
        for h in range(HALVES):
            own = weights * control[:, pl.ds(pl.multiple_of(b * COLS + h * LANES, LANES), LANES)]
            for f in range(2):
                line = jnp.sum(own[f * 16 : (f + 1) * 16], axis=0, keepdims=True)
                static[pl.ds(f * (lines // 2) + HALVES * b + h, 1), :] = line
        return carry

    lax.fori_loop(0, nblk, static_line, 0, unroll=4)


def side_blocks(scale, left, offs, tabs, cnts, halo, perturb, tables, words, part):
    width = perturb.shape[2]
    nblk = width // COLS
    edge = HB * COLS
    words[:, pl.ds(pl.multiple_of(jnp.where(left, 0, width + edge), LANES), edge)] = halo[...]
    first = jnp.where(left, 0, nblk - HB)
    for u in range(HB):
        block_term(
            first + u, nblk + 2 * HB, offs, tabs, cnts, words, tables, perturb, part, scale
        )


def near_kernel(scale, offs, tabs, cnts, halo, perturb, tables, words_in, part_in, words, part):
    del words_in, part_in
    side_blocks(
        scale, jnp.logical_not(far_is_left()), offs, tabs, cnts, halo, perturb, tables, words, part
    )


def far_kernel(scale, offs, tabs, cnts, halo, perturb, tables, words_in, part_in, out, words, part):
    del words_in, part_in
    side_blocks(scale, far_is_left(), offs, tabs, cnts, halo, perturb, tables, words, part)
    lines = out.shape[1]
    groups = lines // 2 // 16

    def pack(i, carry):
        f, g = i // groups, i % groups
        for l0 in (0, 8):
            at = pl.ds(pl.multiple_of(f * 16 + l0, 8), 8)
            block = jnp.swapaxes(part[pl.ds(g * 16, 16), at, :], 0, 1).astype(out.dtype)
            out[l0 : l0 + 8, pl.ds(pl.multiple_of(i * 16, 16), 16), :] = block
        return carry

    lax.fori_loop(0, 2 * groups, pack, 0)


VMEM = pl.BlockSpec(memory_space=pltpu.VMEM)
SMEM = pl.BlockSpec(memory_space=pltpu.SMEM)
ANY = pl.BlockSpec(memory_space=pl.ANY)


def params(mib):
    return pltpu.CompilerParams(vmem_limit_bytes=mib * 2**20)


def cost(flops, nbytes):
    return pl.CostEstimate(flops=flops, bytes_accessed=nbytes, transcendentals=0)


def like(array):
    return pltpu.VMEM(array.shape, array.dtype)


def load(perturb, control, tables, offs, tabs, cnts, cov):
    members, fl, width = perturb.shape
    edge = HB * COLS
    send = pltpu.VMEM((members * fl, edge), jnp.bfloat16)
    words = pltpu.VMEM((members * fl, width + 2 * edge + COLS), jnp.bfloat16)
    scalars = (offs, tabs, cnts, cov)
    copies = 2 * (2 + (width - 2 * edge) // (4 * COLS)) + 2 + len(scalars)
    return pl.pallas_call(
        load_kernel,
        out_shape=(send, send, words, like(perturb), like(control), like(tables))
        + tuple(pltpu.SMEM(x.shape, x.dtype) for x in scalars),
        in_specs=[ANY] * 7,
        out_specs=(VMEM,) * 6 + (SMEM,) * 4,
        scratch_shapes=[pltpu.SemaphoreType.DMA((copies,))],
        compiler_params=params(16),
        cost_estimate=cost(10**6, 12 * 2**20),
    )(*(pltpu.with_memory_space_constraint(x, pltpu.HBM) for x in (perturb, control, tables) + scalars))


def block_cost(perturb, offs, blocks):
    members, fl, _ = perturb.shape
    return cost(2 * members * fl * COLS**2 * offs.shape[0] * blocks, blocks * 2**19)


def inner_blocks(scale, offs, tabs, cnts, cov, words, perturb, control, tables):
    _, fl, width = perturb.shape
    lines = width // LANES
    return pl.pallas_call(
        functools.partial(inner_kernel, scale),
        out_shape=(
            pltpu.VMEM((lines, fl, LANES), jnp.float32),
            pltpu.VMEM((2 * lines, LANES), jnp.float32),
        ),
        in_specs=[SMEM] * 4 + [VMEM] * 4,
        out_specs=(VMEM, VMEM),
        compiler_params=params(16),
        cost_estimate=block_cost(perturb, offs, width // COLS - 2 * HB),
    )(offs, tabs, cnts, cov, words, perturb, control, tables)


def near_blocks(scale, offs, tabs, cnts, halo, perturb, tables, words, part):
    return pl.pallas_call(
        functools.partial(near_kernel, scale),
        out_shape=(like(words), like(part)),
        in_specs=[SMEM] * 3 + [VMEM] * 5,
        out_specs=(VMEM, VMEM),
        input_output_aliases={6: 0, 7: 1},
        compiler_params=params(16),
        cost_estimate=block_cost(perturb, offs, HB),
    )(offs, tabs, cnts, halo, perturb, tables, words, part)


def far_blocks(scale, levels, offs, tabs, cnts, halo, perturb, tables, words, part):
    lines = part.shape[0] * part.shape[1] // levels
    return pl.pallas_call(
        functools.partial(far_kernel, scale),
        out_shape=(pltpu.VMEM((levels, lines, LANES), jnp.bfloat16), like(words), like(part)),
        in_specs=[SMEM] * 3 + [VMEM] * 5,
        out_specs=(VMEM, VMEM, VMEM),
        input_output_aliases={6: 1, 7: 2},
        compiler_params=params(16),
        cost_estimate=block_cost(perturb, offs, HB),
    )(offs, tabs, cnts, halo, perturb, tables, words, part)[0]


def per_device(perturb, control, static_cov, loc_table, pair_offset, pair_table, pair_count):
    groups = lax.axis_size("member")
    bands = lax.axis_size("band")
    members, fields, levels, width = perturb.shape
    scale = 0.5 / (members * groups - 1)
    perturb = perturb.reshape(members, fields * levels, width)
    control = control.reshape(fields * levels, width)
    cov = static_cov.reshape(fields * levels, levels)

    far, near, words, perturb, control, tables, offs, tabs, cnts, cov = load(
        perturb, control, loc_table, pair_offset.T, pair_table.T, pair_count, cov
    )
    across = [(i, (i + (1 if i % 2 else -1)) % bands) for i in range(bands)]
    beside = [(i, i - 1 if i % 2 else i + 1) for i in range(bands)]
    far = lax.ppermute(far, "band", across)
    near = lax.ppermute(near, "band", beside)
    part, static = inner_blocks(scale, offs, tabs, cnts, cov, words, perturb, control, tables)
    words, part = near_blocks(scale, offs, tabs, cnts, near, perturb, tables, words, part)
    partial = far_blocks(scale, levels, offs, tabs, cnts, far, perturb, tables, words, part)
    owned = lax.all_to_all(partial, "member", split_axis=0, concat_axis=0, tiled=True)
    total = jnp.sum(owned.astype(jnp.float32), axis=0) + static
    return total.reshape(fields, 1, width)


def solution(mesh):
    return jax.shard_map(
        per_device,
        mesh=mesh,
        in_specs=(
            P("member", None, None, "band"),
            P(None, None, "band"),
            P(),
            P(),
            P("band", None),
            P("band", None),
            P("band"),
        ),
        out_specs=P(None, "member", "band"),
        check_vma=False,
    )
```

```python
import functools

import jax
import jax.numpy as jnp
from jax import lax
from jax.experimental import pallas as pl
from jax.experimental.pallas import tpu as pltpu
from jax.sharding import PartitionSpec as P

HB = 6
COLS = 256
LANES = 128
HALVES = COLS // LANES
INNER_RUN = 10
AHEAD_FLOPS = 2 * 10**10
INNER_FLOPS = 10**5


def form_words(perturb, control, cols):
    members, fl = perturb.shape[0], perturb.shape[1]
    ctl = control[:, cols]
    return [
        (slice(k * fl, (k + 1) * fl), (perturb[k, :, cols].astype(jnp.float32) * ctl).astype(jnp.bfloat16))
        for k in range(members)
    ]


def block_term(b, zero_block, offs, tabs, cnts, words, tables, perturb, part, scale):
    count = cnts[b]
    acc = None
    for s in range(offs.shape[0]):
        c = jnp.where(s < count, HB + b + offs[s, b], zero_block)
        lhs = words[:, pl.ds(pl.multiple_of(c * COLS, COLS), COLS)]
        prod = jnp.dot(lhs, tables[tabs[s, b]], preferred_element_type=jnp.float32)
        acc = prod if acc is None else acc + prod
    cols = pl.ds(pl.multiple_of(b * COLS, COLS), COLS)
    members, fl = perturb.shape[0], perturb.shape[1]
    total = None
    for k in range(members):
        term = perturb[k, :, cols].astype(jnp.float32) * acc[k * fl : (k + 1) * fl]
        total = term if total is None else total + term
    total = total * scale
    for h in range(HALVES):
        part[HALVES * b + h] = total[:, h * LANES : (h + 1) * LANES]


def far_is_left():
    return lax.axis_index("band") % 2 == 0


def start_all(sems, pairs):
    copies = [pltpu.make_async_copy(src, dst, sems.at[i]) for i, (src, dst) in enumerate(pairs)]
    for copy in copies:
        copy.start()
    return copies


def form_run(lo, size, member_weights, perturb, control, words, static, send=None):
    edge = HB * COLS
    lines = static.shape[0] // 2

    def form(j, carry):
        cols = pl.ds(pl.multiple_of(lo + j * LANES, LANES), LANES)
        dst = pl.ds(pl.multiple_of(edge + lo + j * LANES, LANES), LANES)
        for rows, value in form_words(perturb, control, cols):
            words[rows, dst] = value
            if send is not None:
                send[rows, pl.ds(pl.multiple_of(j * LANES, LANES), LANES)] = value
        own = member_weights * control[:, cols]
        for f in range(2):
            line = jnp.sum(own[f * 16 : (f + 1) * 16], axis=0, keepdims=True)
            static[pl.ds(f * lines + lo // LANES + j, 1), :] = line
        return carry

    lax.fori_loop(0, size // LANES, form, 0, unroll=2)


def static_weights(cov, fl):
    row = lax.broadcasted_iota(jnp.int32, (fl, LANES), 0)
    me = lax.axis_index("member")
    weights = jnp.zeros((fl, LANES), jnp.float32)
    for f in range(2):
        for l in range(16):
            weights = jnp.where(row == f * 16 + l, 0.5 * cov[f * 16 + me, l], weights)
    return weights


def edge_kernel(
    perturb_in, control_in, offs_in, tabs_in, cnts_in, cov_in,
    far, near, words, static, perturb, offs, tabs, cnts, cov, control, sems,
):
    edge = HB * COLS
    _, fl, width = perturb.shape
    left = far_is_left()
    far_lo = pl.multiple_of(jnp.where(left, 0, width - edge), LANES)
    near_lo = pl.multiple_of(jnp.where(left, width - edge, 0), LANES)
    sides = ((far_lo, far), (near_lo, near))
    pairs = [(cov_in, cov)]
    for lo, _ in sides:
        at = pl.ds(lo, edge)
        pairs.append((perturb_in.at[:, :, at], perturb.at[:, :, at]))
        pairs.append((control_in.at[:, at], control.at[:, at]))
    pairs += [(offs_in, offs), (tabs_in, tabs), (cnts_in, cnts)]
    copies = start_all(sems, pairs)
    zero = width + 2 * edge
    words[:, zero : zero + COLS] = jnp.zeros((words.shape[0], COLS), words.dtype)
    copies[0].wait()
    weights = static_weights(cov, fl)
    for i, (lo, send) in enumerate(sides):
        copies[1 + 2 * i].wait()
        copies[2 + 2 * i].wait()
        form_run(lo, edge, weights, perturb, control, words, static, send)
    for copy in copies[5:]:
        copy.wait()


def loads_ahead():
    band = lax.axis_index("band")
    return (band == 0) | (band == 7)


def rest_of_band(cov, perturb_in, control_in, tables_in, words, static, perturb, tables, control, sems):
    edge = HB * COLS
    _, fl, width = perturb.shape
    chunk = 4 * COLS
    starts = range(edge, width - edge, chunk)
    pairs = []
    for lo in starts:
        at = pl.ds(lo, chunk)
        pairs.append((perturb_in.at[:, :, at], perturb.at[:, :, at]))
        pairs.append((control_in.at[:, at], control.at[:, at]))
    half = tables.shape[0] // 2
    for i in range(2):
        pairs.append((tables_in.at[pl.ds(i * half, half)], tables.at[pl.ds(i * half, half)]))
    copies = start_all(sems, pairs)
    weights = static_weights(cov, fl)
    for i, lo in enumerate(starts):
        copies[2 * i].wait()
        copies[2 * i + 1].wait()
        form_run(lo, chunk, weights, perturb, control, words, static)
    for copy in copies[2 * len(starts) :]:
        copy.wait()


def ahead_kernel(
    cov, perturb_in, control_in, tables_in, words_in, static_in, edges_in, far_in,
    words, static, perturb, far, tables, control, sems,
):
    del words_in, static_in, edges_in, far_in, far

    @pl.when(loads_ahead())
    def _():
        rest_of_band(
            cov, perturb_in, control_in, tables_in, words, static, perturb, tables, control, sems
        )


def inner_kernel(
    scale, offs, tabs, cnts, cov, perturb_in, control_in, tables_in, words_in, static_in, edges_in,
    tables_mine, words, static, perturb, tables, part, control, sems,
):
    del words_in, static_in, edges_in, tables_mine

    @pl.when(jnp.logical_not(loads_ahead()))
    def _():
        rest_of_band(
            cov, perturb_in, control_in, tables_in, words, static, perturb, tables, control, sems
        )

    nblk = perturb.shape[2] // COLS

    def step(i, carry):
        for u in range(INNER_RUN):
            block_term(
                HB + i * INNER_RUN + u, nblk + 2 * HB, offs, tabs, cnts,
                words, tables, perturb, part, scale,
            )
        return carry

    lax.fori_loop(0, (nblk - 2 * HB) // INNER_RUN, step, 0)


def side_blocks(scale, left, offs, tabs, cnts, halo, perturb, tables, words, part):
    width = perturb.shape[2]
    nblk = width // COLS
    edge = HB * COLS
    words[:, pl.ds(pl.multiple_of(jnp.where(left, 0, width + edge), LANES), edge)] = halo[...]
    first = jnp.where(left, 0, nblk - HB)
    for u in range(HB):
        block_term(
            first + u, nblk + 2 * HB, offs, tabs, cnts, words, tables, perturb, part, scale
        )


def near_kernel(scale, offs, tabs, cnts, halo, perturb, tables, words_in, part_in, words, part):
    del words_in, part_in
    side_blocks(
        scale, jnp.logical_not(far_is_left()), offs, tabs, cnts, halo, perturb, tables, words, part
    )


def far_kernel(scale, offs, tabs, cnts, halo, perturb, tables, words_in, part_in, out, words, part):
    del words_in, part_in
    side_blocks(scale, far_is_left(), offs, tabs, cnts, halo, perturb, tables, words, part)
    lines = out.shape[1]
    groups = lines // 2 // 16

    def pack(i, carry):
        f, g = i // groups, i % groups
        for l0 in (0, 8):
            at = pl.ds(pl.multiple_of(f * 16 + l0, 8), 8)
            block = jnp.swapaxes(part[pl.ds(g * 16, 16), at, :], 0, 1).astype(out.dtype)
            out[l0 : l0 + 8, pl.ds(pl.multiple_of(i * 16, 16), 16), :] = block
        return carry

    lax.fori_loop(0, 2 * groups, pack, 0)


VMEM = pl.BlockSpec(memory_space=pltpu.VMEM)
SMEM = pl.BlockSpec(memory_space=pltpu.SMEM)
ANY = pl.BlockSpec(memory_space=pl.ANY)


def params(mib):
    return pltpu.CompilerParams(vmem_limit_bytes=mib * 2**20)


def cost(flops, nbytes):
    return pl.CostEstimate(flops=flops, bytes_accessed=nbytes, transcendentals=0)


def like(array):
    return pltpu.VMEM(array.shape, array.dtype)


def in_hbm(*arrays):
    return [pltpu.with_memory_space_constraint(x, pltpu.HBM) for x in arrays]


def band_edges(perturb, control, offs, tabs, cnts, cov):
    members, fl, width = perturb.shape
    edge = HB * COLS
    send = pltpu.VMEM((members * fl, edge), jnp.bfloat16)
    words = pltpu.VMEM((members * fl, width + 2 * edge + COLS), jnp.bfloat16)
    scalars = (offs, tabs, cnts, cov)
    return pl.pallas_call(
        edge_kernel,
        out_shape=(
            send, send, words, pltpu.VMEM((2 * width // LANES, LANES), jnp.float32), like(perturb),
        )
        + tuple(pltpu.SMEM(x.shape, x.dtype) for x in scalars),
        in_specs=[ANY] * 6,
        out_specs=(VMEM,) * 5 + (SMEM,) * 4,
        scratch_shapes=[like(control), pltpu.SemaphoreType.DMA((4 + len(scalars),))],
        compiler_params=params(16),
        cost_estimate=cost(10**6, 3 * 2**20),
    )(*in_hbm(perturb, control, *scalars))


def block_cost(perturb, offs, blocks):
    members, fl, _ = perturb.shape
    return cost(2 * members * fl * COLS**2 * offs.shape[0] * blocks, blocks * 2**19)


def rest_scratch(control):
    copies = 2 * ((control.shape[1] - 2 * HB * COLS) // (4 * COLS)) + 2
    return [like(control), pltpu.SemaphoreType.DMA((copies,))]


def load_ahead(cov, perturb, control, tables, words, static, edges, far):
    return pl.pallas_call(
        ahead_kernel,
        out_shape=(like(words), like(static), like(perturb), like(far), like(tables)),
        in_specs=[SMEM] + [ANY] * 3 + [VMEM] * 4,
        out_specs=(VMEM,) * 5,
        input_output_aliases={4: 0, 5: 1, 6: 2, 7: 3},
        scratch_shapes=rest_scratch(control),
        compiler_params=params(16),
        cost_estimate=cost(AHEAD_FLOPS, 10**4),
    )(cov, *in_hbm(perturb, control, tables), words, static, edges, far)


def inner_blocks(scale, offs, tabs, cnts, cov, perturb, control, tables, words, static, edges, mine):
    _, fl, width = perturb.shape
    return pl.pallas_call(
        functools.partial(inner_kernel, scale),
        out_shape=(
            like(words), like(static), like(perturb), like(tables),
            pltpu.VMEM((width // LANES, fl, LANES), jnp.float32),
        ),
        in_specs=[SMEM] * 4 + [ANY] * 3 + [VMEM] * 4,
        out_specs=(VMEM,) * 5,
        input_output_aliases={7: 0, 8: 1, 9: 2, 10: 3},
        scratch_shapes=rest_scratch(control),
        compiler_params=params(16),
        cost_estimate=cost(INNER_FLOPS, 10**4),
    )(offs, tabs, cnts, cov, *in_hbm(perturb, control, tables), words, static, edges, mine)


def near_blocks(scale, offs, tabs, cnts, halo, perturb, tables, words, part):
    return pl.pallas_call(
        functools.partial(near_kernel, scale),
        out_shape=(like(words), like(part)),
        in_specs=[SMEM] * 3 + [VMEM] * 5,
        out_specs=(VMEM, VMEM),
        input_output_aliases={6: 0, 7: 1},
        compiler_params=params(16),
        cost_estimate=block_cost(perturb, offs, HB),
    )(offs, tabs, cnts, halo, perturb, tables, words, part)


def far_blocks(scale, levels, offs, tabs, cnts, halo, perturb, tables, words, part):
    lines = part.shape[0] * part.shape[1] // levels
    return pl.pallas_call(
        functools.partial(far_kernel, scale),
        out_shape=(pltpu.VMEM((levels, lines, LANES), jnp.bfloat16), like(words), like(part)),
        in_specs=[SMEM] * 3 + [VMEM] * 5,
        out_specs=(VMEM, VMEM, VMEM),
        input_output_aliases={6: 1, 7: 2},
        compiler_params=params(16),
        cost_estimate=block_cost(perturb, offs, HB),
    )(offs, tabs, cnts, halo, perturb, tables, words, part)[0]


def per_device(perturb, control, static_cov, loc_table, pair_offset, pair_table, pair_count):
    groups = lax.axis_size("member")
    bands = lax.axis_size("band")
    members, fields, levels, width = perturb.shape
    scale = 0.5 / (members * groups - 1)
    perturb = perturb.reshape(members, fields * levels, width)
    control = control.reshape(fields * levels, width)
    cov = static_cov.reshape(fields * levels, levels)

    far, near, words, static, edges, offs, tabs, cnts, cov = band_edges(
        perturb, control, pair_offset.T, pair_table.T, pair_count, cov
    )
    across = [(i, (i + (1 if i % 2 else -1)) % bands) for i in range(bands)]
    beside = [(i, i - 1 if i % 2 else i + 1) for i in range(bands)]
    near = lax.ppermute(near, "band", beside)
    whole = (perturb, control, loc_table)
    words, static, edges, far, tables = load_ahead(cov, *whole, words, static, edges, far)
    far = lax.ppermute(far, "band", across)
    words, static, perturb, tables, part = inner_blocks(
        scale, offs, tabs, cnts, cov, *whole, words, static, edges, tables
    )
    words, part = near_blocks(scale, offs, tabs, cnts, near, perturb, tables, words, part)
    partial = far_blocks(scale, levels, offs, tabs, cnts, far, perturb, tables, words, part)
    owned = lax.all_to_all(partial, "member", split_axis=0, concat_axis=0, tiled=True)
    total = jnp.sum(owned.astype(jnp.float32), axis=0) + static
    return total.reshape(fields, 1, width)


def solution(mesh):
    return jax.shard_map(
        per_device,
        mesh=mesh,
        in_specs=(
            P("member", None, None, "band"),
            P(None, None, "band"),
            P(),
            P(),
            P("band", None),
            P("band", None),
            P("band"),
        ),
        out_specs=P(None, "member", "band"),
        check_vma=False,
    )
```

```python
import functools

import jax
import jax.numpy as jnp
from jax import lax
from jax.experimental import pallas as pl
from jax.experimental.pallas import tpu as pltpu
from jax.sharding import PartitionSpec as P

HB = 6
COLS = 256
LANES = 128
HALVES = COLS // LANES
INNER_RUN = 20
AHEAD_FLOPS = 2 * 10**10
INNER_FLOPS = 10**5


def form_words(perturb, control, cols):
    members, fl = perturb.shape[0], perturb.shape[1]
    ctl = control[:, cols]
    return [
        (slice(k * fl, (k + 1) * fl), (perturb[k, :, cols].astype(jnp.float32) * ctl).astype(jnp.bfloat16))
        for k in range(members)
    ]


def block_term(b, zero_block, offs, tabs, cnts, words, tables, perturb, part, scale):
    count = cnts[b]
    acc = None
    for s in range(offs.shape[0]):
        c = jnp.where(s < count, HB + b + offs[s, b], zero_block)
        lhs = words[:, pl.ds(pl.multiple_of(c * COLS, COLS), COLS)]
        prod = jnp.dot(lhs, tables[tabs[s, b]], preferred_element_type=jnp.float32)
        acc = prod if acc is None else acc + prod
    cols = pl.ds(pl.multiple_of(b * COLS, COLS), COLS)
    members, fl = perturb.shape[0], perturb.shape[1]
    total = None
    for k in range(members):
        term = perturb[k, :, cols].astype(jnp.float32) * acc[k * fl : (k + 1) * fl]
        total = term if total is None else total + term
    total = total * scale
    for h in range(HALVES):
        part[HALVES * b + h] = total[:, h * LANES : (h + 1) * LANES]


def far_is_left():
    return lax.axis_index("band") % 2 == 0


def start_all(sems, pairs):
    copies = [pltpu.make_async_copy(src, dst, sems.at[i]) for i, (src, dst) in enumerate(pairs)]
    for copy in copies:
        copy.start()
    return copies


def form_run(lo, size, member_weights, perturb, control, words, static, send=None):
    edge = HB * COLS
    lines = static.shape[0] // 2

    def form(j, carry):
        cols = pl.ds(pl.multiple_of(lo + j * LANES, LANES), LANES)
        dst = pl.ds(pl.multiple_of(edge + lo + j * LANES, LANES), LANES)
        for rows, value in form_words(perturb, control, cols):
            words[rows, dst] = value
            if send is not None:
                send[rows, pl.ds(pl.multiple_of(j * LANES, LANES), LANES)] = value
        own = member_weights * control[:, cols]
        for f in range(2):
            line = jnp.sum(own[f * 16 : (f + 1) * 16], axis=0, keepdims=True)
            static[pl.ds(f * lines + lo // LANES + j, 1), :] = line
        return carry

    lax.fori_loop(0, size // LANES, form, 0, unroll=2)


def static_weights(cov, fl):
    row = lax.broadcasted_iota(jnp.int32, (fl, LANES), 0)
    me = lax.axis_index("member")
    weights = jnp.zeros((fl, LANES), jnp.float32)
    for f in range(2):
        for l in range(16):
            weights = jnp.where(row == f * 16 + l, 0.5 * cov[f * 16 + me, l], weights)
    return weights


def edge_kernel(
    perturb_in, control_in, offs_in, tabs_in, cnts_in, cov_in,
    far, near, words, static, perturb, offs, tabs, cnts, cov, control, sems,
):
    edge = HB * COLS
    _, fl, width = perturb.shape
    left = far_is_left()
    far_lo = pl.multiple_of(jnp.where(left, 0, width - edge), LANES)
    near_lo = pl.multiple_of(jnp.where(left, width - edge, 0), LANES)
    sides = ((far_lo, far), (near_lo, near))
    pairs = [(cov_in, cov)]
    for lo, _ in sides:
        at = pl.ds(lo, edge)
        pairs.append((perturb_in.at[:, :, at], perturb.at[:, :, at]))
        pairs.append((control_in.at[:, at], control.at[:, at]))
    pairs += [(offs_in, offs), (tabs_in, tabs), (cnts_in, cnts)]
    copies = start_all(sems, pairs)
    zero = width + 2 * edge
    words[:, zero : zero + COLS] = jnp.zeros((words.shape[0], COLS), words.dtype)
    copies[0].wait()
    weights = static_weights(cov, fl)
    for i, (lo, send) in enumerate(sides):
        copies[1 + 2 * i].wait()
        copies[2 + 2 * i].wait()
        form_run(lo, edge, weights, perturb, control, words, static, send)
    for copy in copies[5:]:
        copy.wait()


def loads_ahead():
    band = lax.axis_index("band")
    return (band == 0) | (band == 7)


def rest_of_band(cov, perturb_in, control_in, tables_in, words, static, perturb, tables, control, sems):
    edge = HB * COLS
    _, fl, width = perturb.shape
    chunk = 4 * COLS
    starts = range(edge, width - edge, chunk)
    pairs = []
    for lo in starts:
        at = pl.ds(lo, chunk)
        pairs.append((perturb_in.at[:, :, at], perturb.at[:, :, at]))
        pairs.append((control_in.at[:, at], control.at[:, at]))
    half = tables.shape[0] // 2
    for i in range(2):
        pairs.append((tables_in.at[pl.ds(i * half, half)], tables.at[pl.ds(i * half, half)]))
    copies = start_all(sems, pairs)
    weights = static_weights(cov, fl)
    for i, lo in enumerate(starts):
        copies[2 * i].wait()
        copies[2 * i + 1].wait()
        form_run(lo, chunk, weights, perturb, control, words, static)
    for copy in copies[2 * len(starts) :]:
        copy.wait()


def ahead_kernel(
    cov, perturb_in, control_in, tables_in, words_in, static_in, edges_in, far_in,
    words, static, perturb, far, tables, control, sems,
):
    del words_in, static_in, edges_in, far_in, far

    @pl.when(loads_ahead())
    def _():
        rest_of_band(
            cov, perturb_in, control_in, tables_in, words, static, perturb, tables, control, sems
        )


def inner_kernel(
    scale, offs, tabs, cnts, cov, perturb_in, control_in, tables_in, words_in, static_in, edges_in,
    tables_mine, words, static, perturb, tables, part, control, sems,
):
    del words_in, static_in, edges_in, tables_mine

    @pl.when(jnp.logical_not(loads_ahead()))
    def _():
        rest_of_band(
            cov, perturb_in, control_in, tables_in, words, static, perturb, tables, control, sems
        )

    nblk = perturb.shape[2] // COLS

    def step(i, carry):
        for u in range(INNER_RUN):
            block_term(
                HB + i * INNER_RUN + u, nblk + 2 * HB, offs, tabs, cnts,
                words, tables, perturb, part, scale,
            )
        return carry

    lax.fori_loop(0, (nblk - 2 * HB) // INNER_RUN, step, 0)


def side_blocks(scale, left, offs, tabs, cnts, halo, perturb, tables, words, part):
    width = perturb.shape[2]
    nblk = width // COLS
    edge = HB * COLS
    words[:, pl.ds(pl.multiple_of(jnp.where(left, 0, width + edge), LANES), edge)] = halo[...]
    first = jnp.where(left, 0, nblk - HB)
    for u in range(HB):
        block_term(
            first + u, nblk + 2 * HB, offs, tabs, cnts, words, tables, perturb, part, scale
        )


def near_kernel(scale, offs, tabs, cnts, halo, perturb, tables, words_in, part_in, words, part):
    del words_in, part_in
    side_blocks(
        scale, jnp.logical_not(far_is_left()), offs, tabs, cnts, halo, perturb, tables, words, part
    )


def far_kernel(scale, offs, tabs, cnts, halo, perturb, tables, words_in, part_in, out, words, part):
    del words_in, part_in
    side_blocks(scale, far_is_left(), offs, tabs, cnts, halo, perturb, tables, words, part)
    lines = out.shape[1]
    groups = lines // 2 // 16

    def pack(i, carry):
        f, g = i // groups, i % groups
        for l0 in (0, 8):
            at = pl.ds(pl.multiple_of(f * 16 + l0, 8), 8)
            block = jnp.swapaxes(part[pl.ds(g * 16, 16), at, :], 0, 1).astype(out.dtype)
            out[l0 : l0 + 8, pl.ds(pl.multiple_of(i * 16, 16), 16), :] = block
        return carry

    lax.fori_loop(0, 2 * groups, pack, 0)


VMEM = pl.BlockSpec(memory_space=pltpu.VMEM)
SMEM = pl.BlockSpec(memory_space=pltpu.SMEM)
ANY = pl.BlockSpec(memory_space=pl.ANY)


def params(mib):
    return pltpu.CompilerParams(vmem_limit_bytes=mib * 2**20)


def cost(flops, nbytes):
    return pl.CostEstimate(flops=flops, bytes_accessed=nbytes, transcendentals=0)


def like(array):
    return pltpu.VMEM(array.shape, array.dtype)


def in_hbm(*arrays):
    return [pltpu.with_memory_space_constraint(x, pltpu.HBM) for x in arrays]


def band_edges(perturb, control, offs, tabs, cnts, cov):
    members, fl, width = perturb.shape
    edge = HB * COLS
    send = pltpu.VMEM((members * fl, edge), jnp.bfloat16)
    words = pltpu.VMEM((members * fl, width + 2 * edge + COLS), jnp.bfloat16)
    scalars = (offs, tabs, cnts, cov)
    return pl.pallas_call(
        edge_kernel,
        out_shape=(
            send, send, words, pltpu.VMEM((2 * width // LANES, LANES), jnp.float32), like(perturb),
        )
        + tuple(pltpu.SMEM(x.shape, x.dtype) for x in scalars),
        in_specs=[ANY] * 6,
        out_specs=(VMEM,) * 5 + (SMEM,) * 4,
        scratch_shapes=[like(control), pltpu.SemaphoreType.DMA((4 + len(scalars),))],
        compiler_params=params(16),
        cost_estimate=cost(10**6, 3 * 2**20),
    )(*in_hbm(perturb, control, *scalars))


def block_cost(perturb, offs, blocks):
    members, fl, _ = perturb.shape
    return cost(2 * members * fl * COLS**2 * offs.shape[0] * blocks, blocks * 2**19)


def rest_scratch(control):
    copies = 2 * ((control.shape[1] - 2 * HB * COLS) // (4 * COLS)) + 2
    return [like(control), pltpu.SemaphoreType.DMA((copies,))]


def load_ahead(cov, perturb, control, tables, words, static, edges, far):
    return pl.pallas_call(
        ahead_kernel,
        out_shape=(like(words), like(static), like(perturb), like(far), like(tables)),
        in_specs=[SMEM] + [ANY] * 3 + [VMEM] * 4,
        out_specs=(VMEM,) * 5,
        input_output_aliases={4: 0, 5: 1, 6: 2, 7: 3},
        scratch_shapes=rest_scratch(control),
        compiler_params=params(16),
        cost_estimate=cost(AHEAD_FLOPS, 10**4),
    )(cov, *in_hbm(perturb, control, tables), words, static, edges, far)


def inner_blocks(scale, offs, tabs, cnts, cov, perturb, control, tables, words, static, edges, mine):
    _, fl, width = perturb.shape
    return pl.pallas_call(
        functools.partial(inner_kernel, scale),
        out_shape=(
            like(words), like(static), like(perturb), like(tables),
            pltpu.VMEM((width // LANES, fl, LANES), jnp.float32),
        ),
        in_specs=[SMEM] * 4 + [ANY] * 3 + [VMEM] * 4,
        out_specs=(VMEM,) * 5,
        input_output_aliases={7: 0, 8: 1, 9: 2, 10: 3},
        scratch_shapes=rest_scratch(control),
        compiler_params=params(16),
        cost_estimate=cost(INNER_FLOPS, 10**4),
    )(offs, tabs, cnts, cov, *in_hbm(perturb, control, tables), words, static, edges, mine)


def near_blocks(scale, offs, tabs, cnts, halo, perturb, tables, words, part):
    return pl.pallas_call(
        functools.partial(near_kernel, scale),
        out_shape=(like(words), like(part)),
        in_specs=[SMEM] * 3 + [VMEM] * 5,
        out_specs=(VMEM, VMEM),
        input_output_aliases={6: 0, 7: 1},
        compiler_params=params(16),
        cost_estimate=block_cost(perturb, offs, HB),
    )(offs, tabs, cnts, halo, perturb, tables, words, part)


def far_blocks(scale, levels, offs, tabs, cnts, halo, perturb, tables, words, part):
    lines = part.shape[0] * part.shape[1] // levels
    return pl.pallas_call(
        functools.partial(far_kernel, scale),
        out_shape=(pltpu.VMEM((levels, lines, LANES), jnp.bfloat16), like(words), like(part)),
        in_specs=[SMEM] * 3 + [VMEM] * 5,
        out_specs=(VMEM, VMEM, VMEM),
        input_output_aliases={6: 1, 7: 2},
        compiler_params=params(16),
        cost_estimate=block_cost(perturb, offs, HB),
    )(offs, tabs, cnts, halo, perturb, tables, words, part)[0]


def per_device(perturb, control, static_cov, loc_table, pair_offset, pair_table, pair_count):
    groups = lax.axis_size("member")
    bands = lax.axis_size("band")
    members, fields, levels, width = perturb.shape
    scale = 0.5 / (members * groups - 1)
    perturb = perturb.reshape(members, fields * levels, width)
    control = control.reshape(fields * levels, width)
    cov = static_cov.reshape(fields * levels, levels)

    far, near, words, static, edges, offs, tabs, cnts, cov = band_edges(
        perturb, control, pair_offset.T, pair_table.T, pair_count, cov
    )
    across = [(i, (i + (1 if i % 2 else -1)) % bands) for i in range(bands)]
    beside = [(i, i - 1 if i % 2 else i + 1) for i in range(bands)]
    near = lax.ppermute(near, "band", beside)
    whole = (perturb, control, loc_table)
    words, static, edges, far, tables = load_ahead(cov, *whole, words, static, edges, far)
    far = lax.ppermute(far, "band", across)
    words, static, perturb, tables, part = inner_blocks(
        scale, offs, tabs, cnts, cov, *whole, words, static, edges, tables
    )
    words, part = near_blocks(scale, offs, tabs, cnts, near, perturb, tables, words, part)
    partial = far_blocks(scale, levels, offs, tabs, cnts, far, perturb, tables, words, part)
    owned = lax.all_to_all(partial, "member", split_axis=0, concat_axis=0, tiled=True)
    total = jnp.sum(owned.astype(jnp.float32), axis=0) + static
    return total.reshape(fields, 1, width)


def solution(mesh):
    return jax.shard_map(
        per_device,
        mesh=mesh,
        in_specs=(
            P("member", None, None, "band"),
            P(None, None, "band"),
            P(),
            P(),
            P("band", None),
            P("band", None),
            P("band"),
        ),
        out_specs=P(None, "member", "band"),
        check_vma=False,
    )
```

```python
import functools

import jax
import jax.numpy as jnp
from jax import lax
from jax.experimental import pallas as pl
from jax.experimental.pallas import tpu as pltpu
from jax.sharding import PartitionSpec as P

HB = 6
COLS = 256
LANES = 128
HALVES = COLS // LANES
INNER_RUN = 20
AHEAD_FLOPS = 2 * 10**10
INNER_FLOPS = 10**5


def form_words(perturb, control, cols):
    members, fl = perturb.shape[0], perturb.shape[1]
    ctl = control[:, cols]
    return [
        (slice(k * fl, (k + 1) * fl), (perturb[k, :, cols].astype(jnp.float32) * ctl).astype(jnp.bfloat16))
        for k in range(members)
    ]


def block_term(b, zero_block, offs, tabs, cnts, words, tables, perturb, part, scale):
    count = cnts[b]
    acc = None
    for s in range(offs.shape[0]):
        c = jnp.where(s < count, HB + b + offs[s, b], zero_block)
        lhs = words[:, pl.ds(pl.multiple_of(c * COLS, COLS), COLS)]
        prod = jnp.dot(lhs, tables[tabs[s, b]], preferred_element_type=jnp.float32)
        acc = prod if acc is None else acc + prod
    cols = pl.ds(pl.multiple_of(b * COLS, COLS), COLS)
    members, fl = perturb.shape[0], perturb.shape[1]
    total = None
    for k in range(members):
        term = perturb[k, :, cols].astype(jnp.float32) * acc[k * fl : (k + 1) * fl]
        total = term if total is None else total + term
    total = total * scale
    for h in range(HALVES):
        part[HALVES * b + h] = total[:, h * LANES : (h + 1) * LANES]


def far_is_left():
    return lax.axis_index("band") % 2 == 0


def start_all(sems, pairs):
    copies = [pltpu.make_async_copy(src, dst, sems.at[i]) for i, (src, dst) in enumerate(pairs)]
    for copy in copies:
        copy.start()
    return copies


def form_run(lo, size, member_weights, perturb, control, words, static, send=None):
    edge = HB * COLS
    lines = static.shape[0] // 2

    def form(j, carry):
        cols = pl.ds(pl.multiple_of(lo + j * LANES, LANES), LANES)
        dst = pl.ds(pl.multiple_of(edge + lo + j * LANES, LANES), LANES)
        for rows, value in form_words(perturb, control, cols):
            words[rows, dst] = value
            if send is not None:
                send[rows, pl.ds(pl.multiple_of(j * LANES, LANES), LANES)] = value
        own = member_weights * control[:, cols]
        for f in range(2):
            line = jnp.sum(own[f * 16 : (f + 1) * 16], axis=0, keepdims=True)
            static[pl.ds(f * lines + lo // LANES + j, 1), :] = line
        return carry

    lax.fori_loop(0, size // LANES, form, 0, unroll=2)


def static_weights(cov, fl):
    row = lax.broadcasted_iota(jnp.int32, (fl, LANES), 0)
    me = lax.axis_index("member")
    weights = jnp.zeros((fl, LANES), jnp.float32)
    for f in range(2):
        for l in range(16):
            weights = jnp.where(row == f * 16 + l, 0.5 * cov[f * 16 + me, l], weights)
    return weights


def edge_kernel(
    perturb_in, control_in, offs_in, tabs_in, cnts_in, cov_in,
    far, near, words, static, perturb, offs, tabs, cnts, cov, control, sems,
):
    edge = HB * COLS
    _, fl, width = perturb.shape
    left = far_is_left()
    far_lo = pl.multiple_of(jnp.where(left, 0, width - edge), LANES)
    near_lo = pl.multiple_of(jnp.where(left, width - edge, 0), LANES)
    sides = ((far_lo, far), (near_lo, near))
    pairs = [(cov_in, cov)]
    for lo, _ in sides:
        at = pl.ds(lo, edge)
        pairs.append((perturb_in.at[:, :, at], perturb.at[:, :, at]))
        pairs.append((control_in.at[:, at], control.at[:, at]))
    pairs += [(offs_in, offs), (tabs_in, tabs), (cnts_in, cnts)]
    copies = start_all(sems, pairs)
    zero = width + 2 * edge
    words[:, zero : zero + COLS] = jnp.zeros((words.shape[0], COLS), words.dtype)
    copies[0].wait()
    weights = static_weights(cov, fl)
    for i, (lo, send) in enumerate(sides):
        copies[1 + 2 * i].wait()
        copies[2 + 2 * i].wait()
        form_run(lo, edge, weights, perturb, control, words, static, send)
    for copy in copies[5:]:
        copy.wait()


def loads_ahead():
    band = lax.axis_index("band")
    return (band == 0) | (band == 7)


def rest_of_band(cov, perturb_in, control_in, tables_in, words, static, perturb, tables, control, sems):
    edge = HB * COLS
    _, fl, width = perturb.shape
    chunk = 4 * COLS
    starts = range(edge, width - edge, chunk)
    pairs = []
    for lo in starts:
        at = pl.ds(lo, chunk)
        pairs.append((perturb_in.at[:, :, at], perturb.at[:, :, at]))
        pairs.append((control_in.at[:, at], control.at[:, at]))
    half = tables.shape[0] // 2
    for i in range(2):
        pairs.append((tables_in.at[pl.ds(i * half, half)], tables.at[pl.ds(i * half, half)]))
    copies = start_all(sems, pairs)
    weights = static_weights(cov, fl)
    for i, lo in enumerate(starts):
        copies[2 * i].wait()
        copies[2 * i + 1].wait()
        form_run(lo, chunk, weights, perturb, control, words, static)
    for copy in copies[2 * len(starts) :]:
        copy.wait()


def ahead_kernel(
    cov, perturb_in, control_in, tables_in, words_in, static_in, edges_in, far_in,
    words, static, perturb, far, tables, control, sems,
):
    del words_in, static_in, edges_in, far_in, far

    @pl.when(loads_ahead())
    def _():
        rest_of_band(
            cov, perturb_in, control_in, tables_in, words, static, perturb, tables, control, sems
        )


def inner_kernel(
    scale, offs, tabs, cnts, cov, perturb_in, control_in, tables_in, words_in, static_in, edges_in,
    tables_mine, words, static, perturb, tables, part, control, sems,
):
    del words_in, static_in, edges_in, tables_mine

    @pl.when(jnp.logical_not(loads_ahead()))
    def _():
        rest_of_band(
            cov, perturb_in, control_in, tables_in, words, static, perturb, tables, control, sems
        )

    nblk = perturb.shape[2] // COLS

    def step(i, carry):
        for u in range(INNER_RUN):
            block_term(
                HB + i * INNER_RUN + u, nblk + 2 * HB, offs, tabs, cnts,
                words, tables, perturb, part, scale,
            )
        return carry

    lax.fori_loop(0, (nblk - 2 * HB) // INNER_RUN, step, 0)


def side_blocks(scale, left, offs, tabs, cnts, halo, perturb, tables, words, part):
    width = perturb.shape[2]
    nblk = width // COLS
    edge = HB * COLS
    words[:, pl.ds(pl.multiple_of(jnp.where(left, 0, width + edge), LANES), edge)] = halo[...]
    first = jnp.where(left, 0, nblk - HB)
    for u in range(HB):
        block_term(
            first + u, nblk + 2 * HB, offs, tabs, cnts, words, tables, perturb, part, scale
        )


def pack(group, part, out):
    groups = out.shape[1] // 2 // 16
    for f in range(2):
        for l0 in (0, 8):
            block = part[pl.ds(pl.multiple_of(group * 16, 16), 16), f * 16 + l0 : f * 16 + l0 + 8, :]
            rows = pl.ds(pl.multiple_of((f * groups + group) * 16, 16), 16)
            out[l0 : l0 + 8, rows, :] = jnp.swapaxes(block, 0, 1).astype(out.dtype)


def near_kernel(
    scale, offs, tabs, cnts, halo, perturb, tables, words_in, part_in, words, part, out
):
    del words_in, part_in
    groups = out.shape[1] // 2 // 16
    for g in range(1, groups - 1):
        pack(g, part, out)
    left = jnp.logical_not(far_is_left())
    side_blocks(scale, left, offs, tabs, cnts, halo, perturb, tables, words, part)
    pack(jnp.where(left, 0, groups - 1), part, out)


def far_kernel(
    scale, offs, tabs, cnts, halo, perturb, tables, words_in, part_in, out_in, out, words, part
):
    del words_in, part_in, out_in
    left = far_is_left()
    side_blocks(scale, left, offs, tabs, cnts, halo, perturb, tables, words, part)
    pack(jnp.where(left, 0, out.shape[1] // 2 // 16 - 1), part, out)


VMEM = pl.BlockSpec(memory_space=pltpu.VMEM)
SMEM = pl.BlockSpec(memory_space=pltpu.SMEM)
ANY = pl.BlockSpec(memory_space=pl.ANY)


def params(mib):
    return pltpu.CompilerParams(vmem_limit_bytes=mib * 2**20)


def cost(flops, nbytes):
    return pl.CostEstimate(flops=flops, bytes_accessed=nbytes, transcendentals=0)


def like(array):
    return pltpu.VMEM(array.shape, array.dtype)


def in_hbm(*arrays):
    return [pltpu.with_memory_space_constraint(x, pltpu.HBM) for x in arrays]


def band_edges(perturb, control, offs, tabs, cnts, cov):
    members, fl, width = perturb.shape
    edge = HB * COLS
    send = pltpu.VMEM((members * fl, edge), jnp.bfloat16)
    words = pltpu.VMEM((members * fl, width + 2 * edge + COLS), jnp.bfloat16)
    scalars = (offs, tabs, cnts, cov)
    return pl.pallas_call(
        edge_kernel,
        out_shape=(
            send, send, words, pltpu.VMEM((2 * width // LANES, LANES), jnp.float32), like(perturb),
        )
        + tuple(pltpu.SMEM(x.shape, x.dtype) for x in scalars),
        in_specs=[ANY] * 6,
        out_specs=(VMEM,) * 5 + (SMEM,) * 4,
        scratch_shapes=[like(control), pltpu.SemaphoreType.DMA((4 + len(scalars),))],
        compiler_params=params(16),
        cost_estimate=cost(10**6, 3 * 2**20),
    )(*in_hbm(perturb, control, *scalars))


def block_cost(perturb, offs, blocks):
    members, fl, _ = perturb.shape
    return cost(2 * members * fl * COLS**2 * offs.shape[0] * blocks, blocks * 2**19)


def rest_scratch(control):
    copies = 2 * ((control.shape[1] - 2 * HB * COLS) // (4 * COLS)) + 2
    return [like(control), pltpu.SemaphoreType.DMA((copies,))]


def load_ahead(cov, perturb, control, tables, words, static, edges, far):
    return pl.pallas_call(
        ahead_kernel,
        out_shape=(like(words), like(static), like(perturb), like(far), like(tables)),
        in_specs=[SMEM] + [ANY] * 3 + [VMEM] * 4,
        out_specs=(VMEM,) * 5,
        input_output_aliases={4: 0, 5: 1, 6: 2, 7: 3},
        scratch_shapes=rest_scratch(control),
        compiler_params=params(16),
        cost_estimate=cost(AHEAD_FLOPS, 10**4),
    )(cov, *in_hbm(perturb, control, tables), words, static, edges, far)


def inner_blocks(scale, offs, tabs, cnts, cov, perturb, control, tables, words, static, edges, mine):
    _, fl, width = perturb.shape
    return pl.pallas_call(
        functools.partial(inner_kernel, scale),
        out_shape=(
            like(words), like(static), like(perturb), like(tables),
            pltpu.VMEM((width // LANES, fl, LANES), jnp.float32),
        ),
        in_specs=[SMEM] * 4 + [ANY] * 3 + [VMEM] * 4,
        out_specs=(VMEM,) * 5,
        input_output_aliases={7: 0, 8: 1, 9: 2, 10: 3},
        scratch_shapes=rest_scratch(control),
        compiler_params=params(16),
        cost_estimate=cost(INNER_FLOPS, 10**4),
    )(offs, tabs, cnts, cov, *in_hbm(perturb, control, tables), words, static, edges, mine)


def near_blocks(scale, levels, offs, tabs, cnts, halo, perturb, tables, words, part):
    lines = part.shape[0] * part.shape[1] // levels
    return pl.pallas_call(
        functools.partial(near_kernel, scale),
        out_shape=(like(words), like(part), pltpu.VMEM((levels, lines, LANES), jnp.bfloat16)),
        in_specs=[SMEM] * 3 + [VMEM] * 5,
        out_specs=(VMEM,) * 3,
        input_output_aliases={6: 0, 7: 1},
        compiler_params=params(16),
        cost_estimate=block_cost(perturb, offs, HB),
    )(offs, tabs, cnts, halo, perturb, tables, words, part)


def far_blocks(scale, offs, tabs, cnts, halo, perturb, tables, words, part, partial):
    return pl.pallas_call(
        functools.partial(far_kernel, scale),
        out_shape=(like(partial), like(words), like(part)),
        in_specs=[SMEM] * 3 + [VMEM] * 6,
        out_specs=(VMEM,) * 3,
        input_output_aliases={6: 1, 7: 2, 8: 0},
        compiler_params=params(16),
        cost_estimate=block_cost(perturb, offs, HB),
    )(offs, tabs, cnts, halo, perturb, tables, words, part, partial)[0]


def per_device(perturb, control, static_cov, loc_table, pair_offset, pair_table, pair_count):
    groups = lax.axis_size("member")
    bands = lax.axis_size("band")
    members, fields, levels, width = perturb.shape
    scale = 0.5 / (members * groups - 1)
    perturb = perturb.reshape(members, fields * levels, width)
    control = control.reshape(fields * levels, width)
    cov = static_cov.reshape(fields * levels, levels)

    far, near, words, static, edges, offs, tabs, cnts, cov = band_edges(
        perturb, control, pair_offset.T, pair_table.T, pair_count, cov
    )
    across = [(i, (i + (1 if i % 2 else -1)) % bands) for i in range(bands)]
    beside = [(i, i - 1 if i % 2 else i + 1) for i in range(bands)]
    near = lax.ppermute(near, "band", beside)
    whole = (perturb, control, loc_table)
    words, static, edges, far, tables = load_ahead(cov, *whole, words, static, edges, far)
    far = lax.ppermute(far, "band", across)
    words, static, perturb, tables, part = inner_blocks(
        scale, offs, tabs, cnts, cov, *whole, words, static, edges, tables
    )
    words, part, partial = near_blocks(
        scale, levels, offs, tabs, cnts, near, perturb, tables, words, part
    )
    partial = far_blocks(
        scale, offs, tabs, cnts, far, perturb, tables, words, part, partial
    )
    owned = lax.all_to_all(partial, "member", split_axis=0, concat_axis=0, tiled=True)
    total = jnp.sum(owned.astype(jnp.float32), axis=0) + static
    return total.reshape(fields, 1, width)


def solution(mesh):
    return jax.shard_map(
        per_device,
        mesh=mesh,
        in_specs=(
            P("member", None, None, "band"),
            P(None, None, "band"),
            P(),
            P(),
            P("band", None),
            P("band", None),
            P("band"),
        ),
        out_specs=P(None, "member", "band"),
        check_vma=False,
    )
```

```python
import functools

import jax
import jax.numpy as jnp
from jax import lax
from jax.experimental import pallas as pl
from jax.experimental.pallas import tpu as pltpu
from jax.sharding import PartitionSpec as P

HB = 6
COLS = 256
LANES = 128
HALVES = COLS // LANES
INNER_RUN = 20
AHEAD_FLOPS = 2 * 10**10
INNER_FLOPS = 10**5


def form_words(perturb, control, cols):
    members, fl = perturb.shape[0], perturb.shape[1]
    ctl = control[:, cols]
    return [
        (slice(k * fl, (k + 1) * fl), (perturb[k, :, cols].astype(jnp.float32) * ctl).astype(jnp.bfloat16))
        for k in range(members)
    ]


def block_term(b, zero_block, offs, tabs, cnts, words, tables, perturb, part, scale):
    count = cnts[b]
    slots = range(offs.shape[0])
    cs = [jnp.where(s < count, HB + b + offs[s, b], zero_block) for s in slots]
    lhs = jnp.concatenate(
        [words[:, pl.ds(pl.multiple_of(c * COLS, COLS), COLS)] for c in cs], axis=1
    )
    rhs = jnp.concatenate([tables[tabs[s, b]] for s in slots], axis=0)
    acc = jnp.dot(lhs, rhs, preferred_element_type=jnp.float32)
    cols = pl.ds(pl.multiple_of(b * COLS, COLS), COLS)
    members, fl = perturb.shape[0], perturb.shape[1]
    total = None
    for k in range(members):
        term = perturb[k, :, cols].astype(jnp.float32) * acc[k * fl : (k + 1) * fl]
        total = term if total is None else total + term
    total = total * scale
    for h in range(HALVES):
        part[HALVES * b + h] = total[:, h * LANES : (h + 1) * LANES]


def far_is_left():
    return lax.axis_index("band") % 2 == 0


def start_all(sems, pairs):
    copies = [pltpu.make_async_copy(src, dst, sems.at[i]) for i, (src, dst) in enumerate(pairs)]
    for copy in copies:
        copy.start()
    return copies


def form_run(lo, size, member_weights, perturb, control, words, static, send=None):
    edge = HB * COLS
    lines = static.shape[0] // 2

    def form(j, carry):
        cols = pl.ds(pl.multiple_of(lo + j * LANES, LANES), LANES)
        dst = pl.ds(pl.multiple_of(edge + lo + j * LANES, LANES), LANES)
        for rows, value in form_words(perturb, control, cols):
            words[rows, dst] = value
            if send is not None:
                send[rows, pl.ds(pl.multiple_of(j * LANES, LANES), LANES)] = value
        own = member_weights * control[:, cols]
        for f in range(2):
            line = jnp.sum(own[f * 16 : (f + 1) * 16], axis=0, keepdims=True)
            static[pl.ds(f * lines + lo // LANES + j, 1), :] = line
        return carry

    lax.fori_loop(0, size // LANES, form, 0, unroll=2)


def static_weights(cov, fl):
    row = lax.broadcasted_iota(jnp.int32, (fl, LANES), 0)
    me = lax.axis_index("member")
    weights = jnp.zeros((fl, LANES), jnp.float32)
    for f in range(2):
        for l in range(16):
            weights = jnp.where(row == f * 16 + l, 0.5 * cov[f * 16 + me, l], weights)
    return weights


def edge_kernel(
    perturb_in, control_in, offs_in, tabs_in, cnts_in, cov_in,
    far, near, words, static, perturb, offs, tabs, cnts, cov, control, sems,
):
    edge = HB * COLS
    _, fl, width = perturb.shape
    left = far_is_left()
    far_lo = pl.multiple_of(jnp.where(left, 0, width - edge), LANES)
    near_lo = pl.multiple_of(jnp.where(left, width - edge, 0), LANES)
    sides = ((far_lo, far), (near_lo, near))
    pairs = [(cov_in, cov)]
    for lo, _ in sides:
        at = pl.ds(lo, edge)
        pairs.append((perturb_in.at[:, :, at], perturb.at[:, :, at]))
        pairs.append((control_in.at[:, at], control.at[:, at]))
    pairs += [(offs_in, offs), (tabs_in, tabs), (cnts_in, cnts)]
    copies = start_all(sems, pairs)
    zero = width + 2 * edge
    words[:, zero : zero + COLS] = jnp.zeros((words.shape[0], COLS), words.dtype)
    copies[0].wait()
    weights = static_weights(cov, fl)
    for i, (lo, send) in enumerate(sides):
        copies[1 + 2 * i].wait()
        copies[2 + 2 * i].wait()
        form_run(lo, edge, weights, perturb, control, words, static, send)
    for copy in copies[5:]:
        copy.wait()


def loads_ahead():
    band = lax.axis_index("band")
    return (band == 0) | (band == 7)


def rest_of_band(cov, perturb_in, control_in, tables_in, words, static, perturb, tables, control, sems):
    edge = HB * COLS
    _, fl, width = perturb.shape
    chunk = 4 * COLS
    starts = range(edge, width - edge, chunk)
    pairs = []
    for lo in starts:
        at = pl.ds(lo, chunk)
        pairs.append((perturb_in.at[:, :, at], perturb.at[:, :, at]))
        pairs.append((control_in.at[:, at], control.at[:, at]))
    half = tables.shape[0] // 2
    for i in range(2):
        pairs.append((tables_in.at[pl.ds(i * half, half)], tables.at[pl.ds(i * half, half)]))
    copies = start_all(sems, pairs)
    weights = static_weights(cov, fl)
    for i, lo in enumerate(starts):
        copies[2 * i].wait()
        copies[2 * i + 1].wait()
        form_run(lo, chunk, weights, perturb, control, words, static)
    for copy in copies[2 * len(starts) :]:
        copy.wait()


def ahead_kernel(
    cov, perturb_in, control_in, tables_in, words_in, static_in, edges_in, far_in,
    words, static, perturb, far, tables, control, sems,
):
    del words_in, static_in, edges_in, far_in, far

    @pl.when(loads_ahead())
    def _():
        rest_of_band(
            cov, perturb_in, control_in, tables_in, words, static, perturb, tables, control, sems
        )


def inner_kernel(
    scale, offs, tabs, cnts, cov, perturb_in, control_in, tables_in, words_in, static_in, edges_in,
    tables_mine, words, static, perturb, tables, part, control, sems,
):
    del words_in, static_in, edges_in, tables_mine

    @pl.when(jnp.logical_not(loads_ahead()))
    def _():
        rest_of_band(
            cov, perturb_in, control_in, tables_in, words, static, perturb, tables, control, sems
        )

    nblk = perturb.shape[2] // COLS

    def step(i, carry):
        for u in range(INNER_RUN):
            block_term(
                HB + i * INNER_RUN + u, nblk + 2 * HB, offs, tabs, cnts,
                words, tables, perturb, part, scale,
            )
        return carry

    lax.fori_loop(0, (nblk - 2 * HB) // INNER_RUN, step, 0)


def side_blocks(scale, left, offs, tabs, cnts, halo, perturb, tables, words, part):
    width = perturb.shape[2]
    nblk = width // COLS
    edge = HB * COLS
    words[:, pl.ds(pl.multiple_of(jnp.where(left, 0, width + edge), LANES), edge)] = halo[...]
    first = jnp.where(left, 0, nblk - HB)
    for u in range(HB):
        block_term(
            first + u, nblk + 2 * HB, offs, tabs, cnts, words, tables, perturb, part, scale
        )


def pack(group, part, out):
    groups = out.shape[1] // 2 // 16
    for f in range(2):
        for l0 in (0, 8):
            block = part[pl.ds(pl.multiple_of(group * 16, 16), 16), f * 16 + l0 : f * 16 + l0 + 8, :]
            rows = pl.ds(pl.multiple_of((f * groups + group) * 16, 16), 16)
            out[l0 : l0 + 8, rows, :] = jnp.swapaxes(block, 0, 1).astype(out.dtype)


def near_kernel(
    scale, offs, tabs, cnts, halo, perturb, tables, words_in, part_in, words, part, out
):
    del words_in, part_in
    groups = out.shape[1] // 2 // 16
    for g in range(1, groups - 1):
        pack(g, part, out)
    left = jnp.logical_not(far_is_left())
    side_blocks(scale, left, offs, tabs, cnts, halo, perturb, tables, words, part)
    pack(jnp.where(left, 0, groups - 1), part, out)


def far_kernel(
    scale, offs, tabs, cnts, halo, perturb, tables, words_in, part_in, out_in, out, words, part
):
    del words_in, part_in, out_in
    left = far_is_left()
    side_blocks(scale, left, offs, tabs, cnts, halo, perturb, tables, words, part)
    pack(jnp.where(left, 0, out.shape[1] // 2 // 16 - 1), part, out)


VMEM = pl.BlockSpec(memory_space=pltpu.VMEM)
SMEM = pl.BlockSpec(memory_space=pltpu.SMEM)
ANY = pl.BlockSpec(memory_space=pl.ANY)


def params(mib):
    return pltpu.CompilerParams(vmem_limit_bytes=mib * 2**20)


def cost(flops, nbytes):
    return pl.CostEstimate(flops=flops, bytes_accessed=nbytes, transcendentals=0)


def like(array):
    return pltpu.VMEM(array.shape, array.dtype)


def in_hbm(*arrays):
    return [pltpu.with_memory_space_constraint(x, pltpu.HBM) for x in arrays]


def band_edges(perturb, control, offs, tabs, cnts, cov):
    members, fl, width = perturb.shape
    edge = HB * COLS
    send = pltpu.VMEM((members * fl, edge), jnp.bfloat16)
    words = pltpu.VMEM((members * fl, width + 2 * edge + COLS), jnp.bfloat16)
    scalars = (offs, tabs, cnts, cov)
    return pl.pallas_call(
        edge_kernel,
        out_shape=(
            send, send, words, pltpu.VMEM((2 * width // LANES, LANES), jnp.float32), like(perturb),
        )
        + tuple(pltpu.SMEM(x.shape, x.dtype) for x in scalars),
        in_specs=[ANY] * 6,
        out_specs=(VMEM,) * 5 + (SMEM,) * 4,
        scratch_shapes=[like(control), pltpu.SemaphoreType.DMA((4 + len(scalars),))],
        compiler_params=params(16),
        cost_estimate=cost(10**6, 3 * 2**20),
    )(*in_hbm(perturb, control, *scalars))


def block_cost(perturb, offs, blocks):
    members, fl, _ = perturb.shape
    return cost(2 * members * fl * COLS**2 * offs.shape[0] * blocks, blocks * 2**19)


def rest_scratch(control):
    copies = 2 * ((control.shape[1] - 2 * HB * COLS) // (4 * COLS)) + 2
    return [like(control), pltpu.SemaphoreType.DMA((copies,))]


def load_ahead(cov, perturb, control, tables, words, static, edges, far):
    return pl.pallas_call(
        ahead_kernel,
        out_shape=(like(words), like(static), like(perturb), like(far), like(tables)),
        in_specs=[SMEM] + [ANY] * 3 + [VMEM] * 4,
        out_specs=(VMEM,) * 5,
        input_output_aliases={4: 0, 5: 1, 6: 2, 7: 3},
        scratch_shapes=rest_scratch(control),
        compiler_params=params(16),
        cost_estimate=cost(AHEAD_FLOPS, 10**4),
    )(cov, *in_hbm(perturb, control, tables), words, static, edges, far)


def inner_blocks(scale, offs, tabs, cnts, cov, perturb, control, tables, words, static, edges, mine):
    _, fl, width = perturb.shape
    return pl.pallas_call(
        functools.partial(inner_kernel, scale),
        out_shape=(
            like(words), like(static), like(perturb), like(tables),
            pltpu.VMEM((width // LANES, fl, LANES), jnp.float32),
        ),
        in_specs=[SMEM] * 4 + [ANY] * 3 + [VMEM] * 4,
        out_specs=(VMEM,) * 5,
        input_output_aliases={7: 0, 8: 1, 9: 2, 10: 3},
        scratch_shapes=rest_scratch(control),
        compiler_params=params(16),
        cost_estimate=cost(INNER_FLOPS, 10**4),
    )(offs, tabs, cnts, cov, *in_hbm(perturb, control, tables), words, static, edges, mine)


def near_blocks(scale, levels, offs, tabs, cnts, halo, perturb, tables, words, part):
    lines = part.shape[0] * part.shape[1] // levels
    return pl.pallas_call(
        functools.partial(near_kernel, scale),
        out_shape=(like(words), like(part), pltpu.VMEM((levels, lines, LANES), jnp.bfloat16)),
        in_specs=[SMEM] * 3 + [VMEM] * 5,
        out_specs=(VMEM,) * 3,
        input_output_aliases={6: 0, 7: 1},
        compiler_params=params(16),
        cost_estimate=block_cost(perturb, offs, HB),
    )(offs, tabs, cnts, halo, perturb, tables, words, part)


def far_blocks(scale, offs, tabs, cnts, halo, perturb, tables, words, part, partial):
    return pl.pallas_call(
        functools.partial(far_kernel, scale),
        out_shape=(like(partial), like(words), like(part)),
        in_specs=[SMEM] * 3 + [VMEM] * 6,
        out_specs=(VMEM,) * 3,
        input_output_aliases={6: 1, 7: 2, 8: 0},
        compiler_params=params(16),
        cost_estimate=block_cost(perturb, offs, HB),
    )(offs, tabs, cnts, halo, perturb, tables, words, part, partial)[0]


def per_device(perturb, control, static_cov, loc_table, pair_offset, pair_table, pair_count):
    groups = lax.axis_size("member")
    bands = lax.axis_size("band")
    members, fields, levels, width = perturb.shape
    scale = 0.5 / (members * groups - 1)
    perturb = perturb.reshape(members, fields * levels, width)
    control = control.reshape(fields * levels, width)
    cov = static_cov.reshape(fields * levels, levels)

    far, near, words, static, edges, offs, tabs, cnts, cov = band_edges(
        perturb, control, pair_offset.T, pair_table.T, pair_count, cov
    )
    across = [(i, (i + (1 if i % 2 else -1)) % bands) for i in range(bands)]
    beside = [(i, i - 1 if i % 2 else i + 1) for i in range(bands)]
    near = lax.ppermute(near, "band", beside)
    whole = (perturb, control, loc_table)
    words, static, edges, far, tables = load_ahead(cov, *whole, words, static, edges, far)
    far = lax.ppermute(far, "band", across)
    words, static, perturb, tables, part = inner_blocks(
        scale, offs, tabs, cnts, cov, *whole, words, static, edges, tables
    )
    words, part, partial = near_blocks(
        scale, levels, offs, tabs, cnts, near, perturb, tables, words, part
    )
    partial = far_blocks(
        scale, offs, tabs, cnts, far, perturb, tables, words, part, partial
    )
    owned = lax.all_to_all(partial, "member", split_axis=0, concat_axis=0, tiled=True)
    total = jnp.sum(owned.astype(jnp.float32), axis=0) + static
    return total.reshape(fields, 1, width)


def solution(mesh):
    return jax.shard_map(
        per_device,
        mesh=mesh,
        in_specs=(
            P("member", None, None, "band"),
            P(None, None, "band"),
            P(),
            P(),
            P("band", None),
            P("band", None),
            P("band"),
        ),
        out_specs=P(None, "member", "band"),
        check_vma=False,
    )
```
